32 devices in a mesh: row: 8 (over z, x), col: 4 (over y, core).
Axes of the slice: x: 2, y: 2, z: 4, core: 2. Of those that a mesh axis runs over, the one named last changes fastest.
Arguments:
- blocks: bfloat16 [256, 16, 128, 128], P('row', 'col'), may hold values from -0.375 to 0.375
- pattern: int32 [256, 16], replicated, may hold values from 0 to 255, as said below
- owners: int32 [4, 256, 4, 1], P('col', 'row'), may hold values from 0 to 7; in each aligned block of 128 rows (0 to 127, 128 to 255, ..., all dimensions but the last counted through in order) at most 24 rows name the same one
Outputs:
- moved: bfloat16 [4, 8, 192, 128, 128], P('col', 'row')
The draws below stay inside these ranges and needn't reach their ends.
Inputs may be any that keep to these rules, and one draw needn't show every extreme that they name: `pattern`: block row i holds 16 distinct column blocks (i + d) mod 256, by rising d with |d| <= 8, d = 0 among them, in slot order. `owners`: among the 128 entries of one device no value occurs more than 24 times; in some device some value occurs exactly 24 times.
All inputs are finite; a program needn't handle non-finite values.
Results may differ from the reference program's by a relative error of at most 0.0049.
Values may be sent and summed in bfloat16 or wider, within the bound.
A program may use at most 192 MiB of HBM per device.

```python
import math
import jax
import jax.numpy as jnp
import numpy as np
from jax import lax

B = 128
K = 16
RG = 32
NB = 256
W = 8
KS = 4
BLK_DEV = 128
CAP = 24
N_ROW = 8
N_COL = 4


def draw_pattern(key, part):
    dropped = jax.random.randint(jax.random.fold_in(key, 11), (NB,), 0, K, dtype=jnp.int32)
    dropped = dropped + (dropped >= W).astype(jnp.int32)
    slot_ids = jnp.arange(K, dtype=jnp.int32)[None, :]
    candidate = slot_ids + (slot_ids >= dropped[:, None]).astype(jnp.int32)
    offsets = candidate - W
    row_ids = jnp.arange(NB, dtype=jnp.int32)[:, None]
    return ((row_ids + offsets + NB) % NB).astype(jnp.int32)


def block_scale(own_key, dims, cuts, low, top_value):
    gain = 1.0
    for dim, parts in cuts:
        steps = jax.random.uniform(jax.random.fold_in(jax.random.fold_in(own_key, 6), dim), (parts,), jnp.float32, low / len(cuts), top_value / len(cuts))
        gain = gain * jnp.repeat(jnp.exp(steps), dims[dim] // parts).reshape((-1,) + (1,) * (len(dims) - 1 - dim))
    return gain


def shared_out(own_key, own, number, rows, count, top, bound, slope):
    ranking = jax.random.permutation(own_key, count)
    heavy_load, ordinary = shares(count, rows * top, bound, slope, True), shares(count, rows * top, bound, slope, False)
    places = jnp.arange(count)

    def named(lengths, turn):
        used = int((lengths > 0).sum())
        fixed = max(1, used // 4)
        passed = fixed + (places - fixed + turn * (used - fixed)) % max(1, count - fixed)
        return jnp.zeros((count,), jnp.int32).at[ranking[jnp.where(places < fixed, places, passed)]].set(jnp.asarray(lengths, jnp.int32))

    lengths = jnp.where(number % 4 == 0, named(heavy_load, number // 4), named(ordinary, number - number // 4 - 1))
    mixed = jax.random.permutation(jax.random.fold_in(own, 3), count)
    source_of, taker = mixed[0:count // 2 * 2:2], mixed[1:count // 2 * 2:2]
    margin = jnp.minimum(lengths[source_of] - 1, bound - lengths[taker]) // 2
    margin = jnp.where((source_of == ranking[0]) | (taker == ranking[0]) | (lengths[taker] == 0), 0, jnp.maximum(margin, 0))
    passed = jax.random.randint(jax.random.fold_in(own, 4), (count // 2,), 0, 1 << 20) % (margin + 1)
    lengths = lengths.at[source_of].add(-passed).at[taker].add(passed)
    members = jnp.searchsorted(jnp.cumsum(lengths), jnp.arange(rows * top), side="right").astype(jnp.int32)
    table = members.reshape(top, rows).T
    table = table[jax.random.permutation(jax.random.fold_in(own, 1), rows)]
    turn = jax.random.randint(jax.random.fold_in(own, 2), (rows, 1), 0, top)
    return jnp.take_along_axis(table, (jnp.arange(top)[None, :] + turn) % top, axis=1)


def shares(number_of, total, limit, slope, full):
    weights = [(1 << 20) // math.isqrt(grade ** slope) + 1 for grade in range(1, number_of + 1)]
    largest = limit if full else min(limit, max(-(-total // number_of), total * weights[0] // sum(weights)))
    least = 1 if total - largest >= number_of - 1 else 0
    holding, spare = [largest] + [least] * (number_of - 1), total - largest - least * (number_of - 1)
    while spare > 0:
        candidates = [i for i in range(1, number_of) if holding[i] < largest] or [i for i in range(1, number_of) if holding[i] < limit]
        mass, budget = sum([weights[i] for i in candidates]), spare
        for i in candidates:
            extra = min(limit - holding[i], max(1, budget * weights[i] // mass), spare)
            holding[i] = holding[i] + extra
            spare = spare - extra
    return np.array(holding)


def noise(key, dims, scale, reach, cuts=(), kind=jnp.bfloat16):
    entries = jax.random.normal(key, dims, jnp.float32) * scale
    if len(cuts) > 0:
        entries = block_scale(key, dims, cuts, -0.22, 0.18) * entries
    return jnp.clip(entries, min=-reach, max=reach).astype(kind)


def setup_inputs(seed: int = 0) -> dict:
    splits = jax.random.split(jax.random.key(seed), 4)
    blocks = noise(splits[0], (NB, K, B, B), 0.06, 0.375, ((0, 8), (1, 4)))
    pattern = draw_pattern(jax.random.fold_in(splits[3], 71), 0)
    owners_keys = jax.random.split(jax.random.fold_in(splits[2], 1), N_COL * NB * KS // BLK_DEV)
    owners_turns = jax.random.permutation(jax.random.fold_in(splits[2], 3), N_COL * NB * KS // BLK_DEV)
    owners = jax.vmap(lambda own, number: shared_out(jax.random.fold_in(splits[2], 2), own, number, BLK_DEV, N_ROW, 1, CAP, 2))(owners_keys, owners_turns).reshape((N_COL, NB, KS, 1))
    return {"blocks": blocks, "pattern": pattern, "owners": owners}


def pick_table(pattern):
    neighbour_cols = pattern[pattern]
    same_col = neighbour_cols[:, None, :, :] == pattern[:, :, None, None]
    has_match = jnp.any(same_col, axis=-1)
    match_slot = jnp.sum(same_col.astype(jnp.int32) * jnp.arange(K, dtype=jnp.int32), axis=-1)
    return jnp.where(has_match, pattern[:, None, :] * K + match_slot, NB * K).astype(jnp.int32)


def multiply(left, blocks, pick):
    flat_table = jnp.concatenate([blocks.reshape(NB * K, B, B), jnp.zeros((1, B, B), blocks.dtype)], axis=0)

    def per_group(operands):
        left_rows, pick_rows = operands
        picked = flat_table[pick_rows].astype(jnp.float32)
        return jnp.einsum('gtab,gstbc->gsac', left_rows.astype(jnp.float32), picked, precision=lax.Precision.HIGHEST)

    result = lax.map(per_group, (left.reshape(NB // 8, 8, K, B, B), pick.reshape(NB // 8, 8, K, K)))
    return result.reshape(NB, K, B, B)


def reference(blocks, pattern, owners):
    pick = pick_table(pattern)
    squared = multiply(blocks, blocks, pick).astype(jnp.bfloat16)
    cube_term = multiply(squared, blocks, pick)
    result = (3.0 * squared.astype(jnp.float32) - 2.0 * cube_term).astype(jnp.bfloat16)
    per_device = result.reshape(N_ROW, RG, N_COL, KS, B, B).transpose(2, 0, 1, 3, 4, 5)
    per_device = per_device.reshape(N_COL * N_ROW * BLK_DEV, B, B)
    destination = owners.reshape(N_COL, N_ROW, BLK_DEV)
    one_hot = (destination[..., None] == jnp.arange(N_ROW, dtype=jnp.int32)).astype(jnp.int32)
    bucket_rank = jnp.sum((jnp.cumsum(one_hot, axis=2) - 1) * one_hot, axis=-1).astype(jnp.int32)
    bucket_slot = destination * CAP + bucket_rank
    target = jnp.arange(N_ROW, dtype=jnp.int32)[:, None] * CAP + jnp.arange(CAP, dtype=jnp.int32)[None, :]
    slot_match = bucket_slot[:, None, :, None, :] == target[None, :, None, :, None]
    has_source = jnp.any(slot_match, axis=-1)
    source = jnp.sum(slot_match.astype(jnp.int32) * jnp.arange(BLK_DEV, dtype=jnp.int32), axis=-1)
    base_index = (jnp.arange(N_COL, dtype=jnp.int32)[:, None, None, None] * N_ROW
                  + jnp.arange(N_ROW, dtype=jnp.int32)[None, None, :, None]) * BLK_DEV
    flat_index = jnp.where(has_source, base_index + source, N_COL * N_ROW * BLK_DEV).astype(jnp.int32)
    padded = jnp.concatenate([per_device, jnp.zeros((1, B, B), per_device.dtype)], axis=0)
    return padded[flat_index].reshape(N_COL, N_ROW, N_ROW * CAP, B, B)
```

```python
import functools
import math

import jax
import jax.numpy as jnp
from jax import lax
from jax.experimental import pallas as pl
from jax.experimental.pallas import tpu as pltpu
from jax.sharding import PartitionSpec as P


def passed_along(shard, axis, by):
    devices = lax.axis_size(axis)
    return lax.ppermute(shard, axis, [(i, (i + by) % devices) for i in range(devices)])


def window_tables(pattern, start_row, row_count, margin, flat_of, empty):
    nblk, slot_count = pattern.shape
    size = row_count + 2 * margin
    ids = (start_row - margin + jnp.arange(size, dtype=jnp.int32) + nblk) % nblk
    cols = pattern[ids]
    match = cols[:, None, :] == ids[None, :, None]
    flat = jnp.asarray(flat_of, jnp.int32)
    place = jnp.where(
        jnp.any(match, axis=-1), jnp.sum(jnp.where(match, flat[:, None, :], 0), axis=-1), empty
    )
    own = cols[margin : margin + row_count]
    column = (own - start_row + margin + nblk) % nblk
    return place.reshape(-1).astype(jnp.int32), column.reshape(-1).astype(jnp.int32)


def fill_dense(place_ref, held, dense, size, tile):
    def fill_row(w, carry):
        rows = pl.ds(pl.multiple_of(w * tile, tile), tile)
        for c in range(size):
            dense[rows, c * tile : (c + 1) * tile] = held[place_ref[w * size + c]]
        return carry

    lax.fori_loop(0, size, fill_row, 0)


def purify(place_ref, column_ref, dense, squared, final, put, dims):
    row_count, slot_count, reach, margin, tile, empty = dims
    size = row_count + 2 * margin
    group = math.gcd(row_count, 4)
    width = group + 2 * reach
    wide = 2 if width % 2 == 0 else 1
    tiles = width // wide

    def per_group(g, carry):
        first = g * group
        low = margin - reach + first

        def cols_of(lo, hi):
            return pl.ds(pl.multiple_of((low + lo) * tile, tile), (hi - lo) * tile)

        own_rows = pl.ds(pl.multiple_of((margin + first) * tile, tile), group * tile)
        spans = []
        for n in range(tiles):
            klo = max(0, n * wide - reach)
            khi = min(width, (n + 1) * wide + reach)
            spans.append((klo, khi))
        for n, (klo, khi) in enumerate(spans):
            product = jnp.dot(
                dense[own_rows, cols_of(klo, khi)],
                dense[cols_of(klo, khi), cols_of(n * wide, (n + 1) * wide)],
                preferred_element_type=jnp.float32,
            )
            for i in range(group):
                for j in range(wide):
                    at = (margin + first + i) * size + low + n * wide + j
                    kept = (place_ref[at] != empty).astype(jnp.float32)
                    part = product[i * tile : (i + 1) * tile, j * tile : (j + 1) * tile] * kept
                    c = n * wide + j
                    squared[i * tile : (i + 1) * tile, c * tile : (c + 1) * tile] = part.astype(
                        squared.dtype
                    )
        for n, (klo, khi) in enumerate(spans):
            cube = jnp.dot(
                squared[:, klo * tile : khi * tile],
                dense[cols_of(klo, khi), cols_of(n * wide, (n + 1) * wide)],
                preferred_element_type=jnp.float32,
            )
            own = squared[:, n * wide * tile : (n + 1) * wide * tile].astype(jnp.float32)
            value = (3.0 * own - 2.0 * cube).astype(final.dtype)
            for j in range(wide):
                final[n * wide + j] = value[:, j * tile : (j + 1) * tile]
        for i in range(group):
            for s in range(slot_count):
                c = column_ref[(first + i) * slot_count + s] - low
                put(first + i, s, final[c, i * tile : (i + 1) * tile, :])
        return carry

    lax.fori_loop(0, row_count // group, per_group, 0)


def local_kernel(dims, place_ref, column_ref, held, out_ref, dense, squared, final):
    row_count, slot_count, reach, margin, tile, empty = dims
    fill_dense(place_ref, held, dense, row_count + 2 * margin, tile)

    def put(i, s, value):
        out_ref[i, s] = value

    purify(place_ref, column_ref, dense, squared, final, put, dims)


def per_device(blocks, pattern, owners):
    row_count, slot_share, tile_size = (blocks.shape[0], blocks.shape[1], blocks.shape[-1])
    slot_count = pattern.shape[1]
    reach = slot_count // 2
    row_pos = lax.axis_index("row")
    col_pos = lax.axis_index("col")
    row_devices = lax.axis_size("row")
    col_devices = lax.axis_size("col")
    row_blocks = lax.all_to_all(blocks, "col", split_axis=0, concat_axis=1, tiled=True)
    local_rows = row_blocks.shape[0]
    hop_count = -(-reach // local_rows)
    lower_list = []
    upper_list = []
    for distance in range(1, hop_count + 1):
        lower_list.append(passed_along(row_blocks, ("row", "col"), distance))
        upper_list.append(passed_along(row_blocks, ("row", "col"), -distance))
    margin = hop_count * local_rows
    size = local_rows + 2 * margin
    empty = size * slot_count
    held = jnp.concatenate(
        [
            part.reshape(-1, tile_size, tile_size)
            for part in lower_list[::-1] + [row_blocks] + upper_list
        ]
        + [jnp.zeros((1, tile_size, tile_size), blocks.dtype)],
        axis=0,
    )
    start_row = (row_pos * col_devices + col_pos) * local_rows
    flat_of = [[w * slot_count + t for t in range(slot_count)] for w in range(size)]
    place, column = window_tables(pattern, start_row, local_rows, margin, flat_of, empty)
    dims = (local_rows, slot_count, reach, margin, tile_size, empty)
    group = math.gcd(local_rows, 4)
    width = group + 2 * reach
    vmem = pl.BlockSpec(memory_space=pltpu.VMEM)
    smem = pl.BlockSpec(memory_space=pltpu.SMEM)
    result_rows = pl.pallas_call(
        functools.partial(local_kernel, dims),
        out_shape=jax.ShapeDtypeStruct(row_blocks.shape, jnp.bfloat16),
        in_specs=[smem, smem, vmem],
        out_specs=vmem,
        scratch_shapes=[
            pltpu.VMEM((size * tile_size, size * tile_size), jnp.bfloat16),
            pltpu.VMEM((group * tile_size, width * tile_size), jnp.bfloat16),
            pltpu.VMEM((width, group * tile_size, tile_size), jnp.bfloat16),
        ],
        compiler_params=pltpu.CompilerParams(vmem_limit_bytes=56 * 2**20),
    )(place, column, held)
    result = lax.all_to_all(result_rows, "col", split_axis=1, concat_axis=0, tiled=True)
    block_count = row_count * slot_share
    capacity = 3 * block_count // (2 * row_devices)
    flat_result = result.reshape(block_count, tile_size, tile_size)
    destination = owners.reshape(block_count)
    one_hot = (destination[:, None] == jnp.arange(row_devices, dtype=jnp.int32)[None, :]).astype(
        jnp.int32
    )
    bucket_rank = jnp.sum((jnp.cumsum(one_hot, axis=0) - 1) * one_hot, axis=1)
    bucket_slot = destination * capacity + bucket_rank
    wanted = jnp.arange(row_devices * capacity, dtype=jnp.int32)
    slot_match = bucket_slot[None, :] == wanted[:, None]
    has_source = jnp.any(slot_match, axis=1)
    source = jnp.sum(
        slot_match.astype(jnp.int32) * jnp.arange(block_count, dtype=jnp.int32)[None, :], axis=1
    )
    padded = jnp.concatenate(
        [flat_result, jnp.zeros((1, tile_size, tile_size), flat_result.dtype)], axis=0
    )
    buckets = padded[jnp.where(has_source, source, block_count)].reshape(
        row_devices, capacity, tile_size, tile_size
    )
    received = lax.all_to_all(buckets, "row", split_axis=0, concat_axis=0, tiled=True)
    return received.reshape(1, 1, row_devices * capacity, tile_size, tile_size)


def solution(mesh):
    in_specs = (P("row", "col", None, None), P(), P("col", "row", None, None))
    out_specs = P("col", "row", None, None, None)
    return jax.shard_map(
        per_device, mesh=mesh, in_specs=in_specs, out_specs=out_specs, check_vma=False
    )
```
